256 devices in a mesh: rows: 32 (over x, z_lo, y), vocab: 8 (over z_hi, core).
Axes of the slice: x: 4, y: 4, z: 8 (z_hi: 4, z_lo: 2; z = z_hi * 2 + z_lo), core: 2. Of those that a mesh axis runs over, the one named last changes fastest.
Arguments:
- teacher_hidden: bfloat16 [512, 4096], P(('rows', 'vocab')), may hold values from -48 to 48
- student_hidden: bfloat16 [512, 2048], P(('rows', 'vocab')), may hold values from -48 to 48
- teacher_head: bfloat16 [151552, 4096], P(('rows', 'vocab')), may hold values from -1 to 1
- student_head: bfloat16 [151552, 2048], P(('rows', 'vocab')), may hold values from -1 to 1
- loss_weight: float32 [512], P(('rows', 'vocab')), may hold values from 0.5 to 4
Outputs:
- student_hidden_grad: float32 [512, 2048], P(('rows', 'vocab'))
- student_head_grad: bfloat16 [151552, 2048], P(('rows', 'vocab'))
The draws below stay inside these ranges and needn't reach their ends.
All inputs are finite; a program needn't handle non-finite values.
Results may differ from the reference program's by a relative error of at most 0.022.
Values may be sent and summed in bfloat16 or wider, within the bound.
No kernel may reach another device: no remote copies, remote signals or barrier semaphores. Data moves between devices by JAX's collectives and lax.ppermute only.
A program may use at most 64 MiB of HBM per device.

```python
import math
import jax
import jax.numpy as jnp
from jax import lax

DT = 4096
DS = 2048
V = 151552
TOKENS = 512


def head_matrix(key, salt, width):
    normal_rows = jax.random.normal(jax.random.fold_in(key, salt), (V, width), jnp.float32)
    scaled = jnp.clip(normal_rows, -4.0, 4.0) / math.sqrt(width)
    return scaled.astype(jnp.bfloat16).astype(jnp.float32)


def draw_teacher_head(key, part):
    return head_matrix(key, 11, DT).astype(jnp.bfloat16)


def draw_student_head(key, part):
    return head_matrix(key, 12, DS).astype(jnp.bfloat16)


def draw_teacher_hidden(key, part):
    inner = jax.random.fold_in(key, 3)
    base = 4.0 * jnp.clip(jax.random.normal(inner, (TOKENS, DT), jnp.float32), -3.0, 3.0)
    return jnp.clip(base, -48.0, 48.0).astype(jnp.bfloat16)


def draw_student_hidden(key, part):
    inner = jax.random.fold_in(key, 4)
    base = 4.0 * jnp.clip(jax.random.normal(inner, (TOKENS, DS), jnp.float32), -3.0, 3.0)
    return jnp.clip(base, -48.0, 48.0).astype(jnp.bfloat16)


def block_levels(own_key, dims, pieces, low, largest):
    def one(axis_at, parts):
        steps = jax.random.uniform(jax.random.fold_in(jax.random.fold_in(own_key, 6), axis_at), (parts,), jnp.float32, low / len(pieces), largest / len(pieces))
        return jnp.repeat(jnp.exp(steps), dims[axis_at] // parts).reshape((-1,) + (1,) * (len(dims) - axis_at - 1))

    level = one(*pieces[0])
    for cut in pieces[1:]:
        level = level * one(*cut)
    return level


def setup_inputs(seed: int = 0) -> dict:
    seeds = jax.random.split(jax.random.key(seed), 6)
    teacher_hidden = draw_teacher_hidden(jax.random.fold_in(seeds[5], 71), 0)
    student_hidden = draw_student_hidden(jax.random.fold_in(seeds[5], 71), 0)
    teacher_head = draw_teacher_head(jax.random.fold_in(seeds[5], 71), 0)
    student_head = draw_student_head(jax.random.fold_in(seeds[5], 71), 0)
    loss_weight = jnp.clip(jnp.exp(math.log(4.0) - 2.0794415 * jax.random.uniform(seeds[4], (TOKENS,), jnp.float32) ** block_levels(seeds[4], (TOKENS,), ((0, 256),), -0.2, 0.2)), 0.5, 4.0)
    return dict(teacher_hidden=teacher_hidden, student_hidden=student_hidden, teacher_head=teacher_head, student_head=student_head, loss_weight=loss_weight)


def row_logits(hidden, head):
    return lax.dot_general(hidden, head, (((1,), (1,)), ((), ())), preferred_element_type=jnp.float32)


def reference(teacher_hidden, student_hidden, teacher_head, student_head, loss_weight):
    block = V // 32
    teach_blocks = teacher_head.reshape(32, block, DT)
    stud_blocks = student_head.reshape(32, block, DS)

    def stat_step(carry, heads):
        peak_teach, total_teach, peak_stud, total_stud = carry
        logit_teach = row_logits(teacher_hidden, heads[0])
        logit_stud = row_logits(student_hidden, heads[1])
        new_teach = jnp.maximum(peak_teach, jnp.max(logit_teach, axis=1))
        new_stud = jnp.maximum(peak_stud, jnp.max(logit_stud, axis=1))
        total_teach = total_teach * jnp.exp(peak_teach - new_teach) + jnp.sum(jnp.exp(logit_teach - new_teach[:, None]), axis=1)
        total_stud = total_stud * jnp.exp(peak_stud - new_stud) + jnp.sum(jnp.exp(logit_stud - new_stud[:, None]), axis=1)
        return (new_teach, total_teach, new_stud, total_stud), None

    lowest = jnp.full((TOKENS,), -jnp.inf, jnp.float32)
    nought = jnp.zeros((TOKENS,), jnp.float32)
    stats, unused = lax.scan(stat_step, (lowest, nought, lowest, nought), (teach_blocks, stud_blocks))
    lse_teach = stats[0] + jnp.log(stats[1])
    lse_stud = stats[2] + jnp.log(stats[3])

    def grad_step(accum, heads):
        logit_teach = row_logits(teacher_hidden, heads[0])
        logit_stud = row_logits(student_hidden, heads[1])
        logit_grad = (loss_weight[:, None] * (jnp.exp(logit_stud - lse_stud[:, None]) - jnp.exp(logit_teach - lse_teach[:, None]))).astype(jnp.bfloat16)
        head_grad = lax.dot_general(logit_grad, student_hidden, (((0,), (0,)), ((), ())), preferred_element_type=jnp.float32).astype(jnp.bfloat16)
        accum = accum + jnp.dot(logit_grad, heads[1], preferred_element_type=jnp.float32)
        return accum, head_grad

    accum, head_grads = lax.scan(grad_step, jnp.zeros((TOKENS, DS), jnp.float32), (teach_blocks, stud_blocks))
    return accum, head_grads.reshape(V, DS)
```

```python
import jax
import jax.numpy as jnp
from jax import lax
from jax.sharding import Mesh, PartitionSpec as P

AXES = ("x", "zl", "y", "zh", "c")
SIZES = (4, 2, 4, 4, 2)
PLANE, LINE, PAIR = ("x", "y"), ("zl", "zh"), ("c",)
NP, NL = 16, 8


def share(block, axes, n):
    return lax.all_to_all(
        jnp.broadcast_to(block[None], (n,) + block.shape), axes, 0, 0, tiled=True
    )


def swap(block):
    return lax.ppermute(block, PAIR, [(0, 1), (1, 0)])


def logits_of(head, hidden):
    return lax.dot_general(
        head, hidden, (((1,), (1,)), ((), ())), preferred_element_type=jnp.float32
    )


def join(stats):
    peak_t, total_t, peak_s, total_s, weight = (stats[:, i] for i in range(5))
    top_t, top_s = jnp.max(peak_t, 0), jnp.max(peak_s, 0)
    return jnp.stack(
        [
            top_t,
            jnp.sum(total_t * jnp.exp(peak_t - top_t), 0),
            top_s,
            jnp.sum(total_s * jnp.exp(peak_s - top_s), 0),
            jnp.sum(weight, 0),
        ]
    )


def on_device(teacher_hidden, student_hidden, teacher_head, student_head, loss_weight):
    tok, dt = teacher_hidden.shape
    ds = student_hidden.shape[1]
    nt = tok * NP * NL
    th = (teacher_head, swap(teacher_head))
    sh = (student_head, swap(student_head))

    mine = jnp.concatenate([teacher_hidden, student_hidden], 1)
    line = share(mine, LINE, NL).reshape(NL * tok, dt + ds)
    hidden = share(line, PLANE, NP).reshape(nt, dt + ds)
    teach, stud = hidden[:, :dt], hidden[:, dt:]

    lt = [logits_of(h, teach) for h in th]
    ls = [logits_of(h, stud) for h in sh]
    peak_t = jnp.maximum(jnp.max(lt[0], 0), jnp.max(lt[1], 0))
    peak_s = jnp.maximum(jnp.max(ls[0], 0), jnp.max(ls[1], 0))
    et = [jnp.exp(v - peak_t) for v in lt]
    es = [jnp.exp(v - peak_s) for v in ls]
    sum_t = jnp.sum(et[0], 0) + jnp.sum(et[1], 0)
    sum_s = jnp.sum(es[0], 0) + jnp.sum(es[1], 0)

    spot = (
        lax.axis_index("x") * 4 + lax.axis_index("y")
    ) * NL + lax.axis_index("zl") * 4 + lax.axis_index("zh")
    weight = lax.dynamic_update_slice(
        jnp.zeros((nt,), jnp.float32), loss_weight, (spot * tok,)
    )
    stats = jnp.stack([peak_t, sum_t, peak_s, sum_s, weight])
    stats = join(share(stats, PLANE, NP))
    stats = join(share(stats, LINE, NL))
    lse_t = stats[0] + jnp.log(stats[1])
    lse_s = stats[2] + jnp.log(stats[3])
    scale_t = stats[4] * jnp.exp(peak_t - lse_t)
    scale_s = stats[4] * jnp.exp(peak_s - lse_s)
    grad = [(s * scale_s - t * scale_t).astype(jnp.bfloat16) for s, t in zip(es, et)]

    theirs = swap(jnp.dot(grad[1], stud, preferred_element_type=jnp.float32))
    part = sum(
        lax.dot_general(
            g, h, (((0,), (0,)), ((), ())), preferred_element_type=jnp.float32
        )
        for g, h in zip(grad, sh)
    )
    part = lax.all_to_all(part.reshape(NP, NL * tok, ds), PLANE, 0, 0, tiled=True)
    part = jnp.sum(part, 0).reshape(NL, tok, ds)
    part = lax.all_to_all(part, LINE, 0, 0, tiled=True)
    hidden_grad = jnp.sum(part, 0)
    head_grad = (
        jnp.dot(grad[0], stud, preferred_element_type=jnp.float32) + theirs
    ).astype(jnp.bfloat16)
    return hidden_grad, head_grad


def solution(mesh):
    fine = Mesh(mesh.devices.reshape(SIZES), AXES)
    split = P(AXES, None)
    return jax.shard_map(
        on_device,
        mesh=fine,
        in_specs=(split, split, split, split, P(AXES)),
        out_specs=(split, split),
        check_vma=False,
    )
```

```python
import jax
import jax.numpy as jnp
from jax import lax
from jax.experimental import pallas as pl
from jax.experimental.pallas import tpu as pltpu
from jax.sharding import Mesh, PartitionSpec as P

AXES = ("x", "zl", "y", "zh", "c")
SIZES = (4, 2, 4, 4, 2)
PLANE, LINE, PAIR = ("x", "y"), ("zl", "zh"), ("c",)
NP, NL = 16, 8
STEPS = (0, 1, 3, 2)
VMEM_LIMIT = 16 * 2**20
WIDE = 2048


def share(block, axes, n):
    return lax.all_to_all(
        jnp.broadcast_to(block[None], (n,) + block.shape), axes, 0, 0, tiled=True
    )


def ring(block, axis):
    return [block] + [
        lax.ppermute(block, axis, [(i, (i + step) % 4) for i in range(4)])
        for step in STEPS[1:]
    ]


def plane_sum(blocks, axes):
    got = lax.all_to_all(blocks, axes, 0, 0, tiled=True)
    return jnp.sum(got.astype(jnp.float32), 0)


def swap(block):
    return lax.ppermute(block, PAIR, [(0, 1), (1, 0)])


def join(stats):
    logs, weight = stats[:, :2], stats[:, 2]
    top = jnp.max(logs, 0)
    logs = top + jnp.log(jnp.sum(jnp.exp(logs - top), 0))
    return jnp.concatenate([logs, jnp.sum(weight, 0)[None]])


def logits_kernel(at, *refs):
    first, second = refs[:4], refs[4:8]
    heads = refs[8:12]
    teach_out, stud_out, stats_out, rows_out = refs[12:16]
    hidden, sem = refs[16:]
    x, y = at[0], at[1]
    half = first[0].shape[2]
    copies = []
    for k in range(4):
        for j in range(4):
            for which, src, dx, dy in (
                (0, first[k], STEPS[j], STEPS[k]),
                (1, second[k], STEPS[k], STEPS[j]),
            ):
                row = ((x - dx) % 4 * 4 + (y - dy) % 4) * 16
                copies.append(
                    pltpu.make_async_copy(
                        src.at[j],
                        hidden.at[pl.ds(row, 16), pl.ds(which * half, half)],
                        sem.at[(k * 4 + j) * 2 + which],
                    )
                )
    for copy in copies:
        copy.start()
    for copy in copies:
        copy.wait()
    rows_out[...] = hidden[:, 2 * WIDE :]
    for h in range(2):
        for out, head, lo in ((teach_out, heads[h], 0), (stud_out, heads[2 + h], 2 * WIDE)):
            out[h] = lax.dot_general(
                head[...],
                hidden[:, lo : lo + head.shape[1]],
                (((1,), (1,)), ((), ())),
                preferred_element_type=jnp.float32,
            )
    for i, out in enumerate((teach_out, stud_out)):
        peak = jnp.max(jnp.max(out[...], 0), 0, keepdims=True)
        terms = jnp.exp(out[...] - peak)
        out[...] = terms
        stats_out[2 * i : 2 * i + 1] = peak
        stats_out[2 * i + 1 : 2 * i + 2] = jnp.sum(jnp.sum(terms, 0), 0, keepdims=True)


def logits(at, first, second, heads):
    ve, nt = heads[0].shape[0], NP * 16
    shape = jax.ShapeDtypeStruct
    return pl.pallas_call(
        logits_kernel,
        out_shape=[
            shape((2, ve, nt), jnp.float32),
            shape((2, ve, nt), jnp.float32),
            shape((4, nt), jnp.float32),
            shape((nt, WIDE), jnp.bfloat16),
        ],
        in_specs=[pl.BlockSpec(memory_space=pltpu.SMEM)]
        + [pl.BlockSpec(memory_space=pl.ANY)] * 8
        + [pl.BlockSpec(memory_space=pltpu.VMEM)] * 4,
        out_specs=[pl.BlockSpec(memory_space=pltpu.VMEM)] * 4,
        scratch_shapes=[
            pltpu.VMEM((nt, 3 * WIDE), jnp.bfloat16),
            pltpu.SemaphoreType.DMA((32,)),
        ],
        compiler_params=pltpu.CompilerParams(vmem_limit_bytes=VMEM_LIMIT),
        cost_estimate=pl.CostEstimate(
            flops=2 * 2 * ve * nt * 3 * WIDE,
            bytes_accessed=2 * ve * 3 * WIDE * 2 + nt * 3 * WIDE * 2,
            transcendentals=4 * ve * nt,
        ),
    )(at, *first, *second, *heads)


def grad_kernel(teach, stud, scale, head0, head1, grad_out, part_out):
    for h in range(2):
        grad_out[h] = (stud[h] * scale[1:2] - teach[h] * scale[0:1]).astype(jnp.bfloat16)
    for n in range(0, WIDE, 512):
        total = sum(
            lax.dot_general(
                grad_out[h],
                head[:, n : n + 512],
                (((0,), (0,)), ((), ())),
                preferred_element_type=jnp.float32,
            )
            for h, head in enumerate((head0, head1))
        )
        part_out[:, n : n + 512] = total.astype(part_out.dtype)


def grads(teach, stud, scale, head0, head1):
    ve, nt = teach.shape[1:]
    shape = jax.ShapeDtypeStruct
    vmem = pl.BlockSpec(memory_space=pltpu.VMEM)
    return pl.pallas_call(
        grad_kernel,
        out_shape=[
            shape((2, ve, nt), jnp.bfloat16),
            shape((nt, WIDE), jnp.bfloat16),
        ],
        in_specs=[vmem] * 5,
        out_specs=[vmem] * 2,
        compiler_params=pltpu.CompilerParams(vmem_limit_bytes=VMEM_LIMIT),
        cost_estimate=pl.CostEstimate(
            flops=2 * 2 * ve * nt * WIDE,
            bytes_accessed=2 * ve * WIDE * 2 + 2 * 2 * ve * nt * 4,
            transcendentals=0,
        ),
    )(teach, stud, scale, head0, head1)


def on_device(teacher_hidden, student_hidden, teacher_head, student_head, loss_weight):
    tok, dt = teacher_hidden.shape
    ds = student_hidden.shape[1]
    nt = tok * NP * NL
    heads = (teacher_head, swap(teacher_head), student_head, swap(student_head))

    x, y = lax.axis_index("x"), lax.axis_index("y")
    mine = jnp.concatenate([teacher_hidden, student_hidden], 1)
    line = share(mine, LINE, NL).reshape(NL * tok, dt + ds)
    line, heads = lax.optimization_barrier((line, heads))
    half = (dt + ds) // 2
    first = ring(jnp.stack(ring(line[:, :half], "x")), "y")
    second = ring(jnp.stack(ring(line[:, half:], "y")), "x")
    teach, stud, stats, rows = logits(jnp.stack([x, y]), first, second, heads)

    z = lax.axis_index("zl") * 4 + lax.axis_index("zh")
    spot = (x * 4 + y) * NL + z
    weight = lax.dynamic_update_slice(
        jnp.zeros((nt,), jnp.float32), loss_weight, (spot * tok,)
    )
    peak, total = stats[0::2], stats[1::2]
    both = jnp.concatenate([peak + jnp.log(total), weight[None]])
    both = join(share(join(share(both, PLANE, NP)), LINE, NL))
    scale = both[2] * jnp.exp(peak - both[:2])
    grad, part = grads(teach, stud, scale, heads[2], heads[3])

    (rows, grad), part = lax.optimization_barrier(((rows, grad), part))
    part = plane_sum(part.reshape(NP, NL * tok, ds), PLANE).reshape(NL, tok, ds)
    theirs = swap(jnp.dot(grad[1], rows, preferred_element_type=jnp.float32))
    ours = jnp.dot(grad[0], rows, preferred_element_type=jnp.float32)
    part, ours, theirs = lax.optimization_barrier((part, ours, theirs))
    hidden_grad = plane_sum(part, LINE)
    return hidden_grad, (ours + theirs).astype(jnp.bfloat16)


def solution(mesh):
    fine = Mesh(mesh.devices.reshape(SIZES), AXES)
    split = P(AXES, None)
    return jax.shard_map(
        on_device,
        mesh=fine,
        in_specs=(split, split, split, split, P(AXES)),
        out_specs=(split, split),
        check_vma=False,
    )
```

```python
import jax
import jax.numpy as jnp
from jax import lax
from jax.experimental import pallas as pl
from jax.experimental.pallas import tpu as pltpu
from jax.sharding import Mesh, PartitionSpec as P

AXES = ("x", "zl", "y", "zh", "c")
SIZES = (4, 2, 4, 4, 2)
PLANE, LINE, PAIR = ("x", "y"), ("zl", "zh"), ("c",)
NP, NL = 16, 8
STEPS = (0, 1, 3, 2)
VMEM_LIMIT = 62 * 2**20
HBM, SMEM = pl.BlockSpec(memory_space=pltpu.HBM), pl.BlockSpec(memory_space=pltpu.SMEM)
VMEM = pl.BlockSpec(memory_space=pltpu.VMEM)
WIDE = 2048


def share(block, axes, n):
    return lax.all_to_all(
        jnp.broadcast_to(block[None], (n,) + block.shape), axes, 0, 0, tiled=True
    )


def ring(block, axis):
    return [block] + [
        lax.ppermute(block, axis, [(i, (i + step) % 4) for i in range(4)])
        for step in STEPS[1:]
    ]


def join(rows, nt):
    logs = rows[:, :, : 2 * nt]
    top = jnp.max(logs, 0)
    logs = top + jnp.log(jnp.sum(jnp.exp(logs - top), 0))
    return jnp.concatenate([logs, jnp.sum(rows[:, :, 2 * nt :], 0)], 1)


def plane_sum(blocks, axes):
    got = lax.all_to_all(blocks, axes, 0, 0, tiled=True)
    return jnp.sum(got.astype(jnp.float32), 0)


def swap(block):
    return lax.ppermute(block, PAIR, [(0, 1), (1, 0)])


def logits_kernel(at, weight, *refs):
    first, second = refs[:4], refs[4:8]
    heads = refs[8:12]
    teach_out, stud_out, rows_out, logs_out, base_out = refs[12:17]
    hidden, held, terms, sem, out_sem = refs[17:]
    x, y = at[0], at[1]
    half = WIDE // 2
    copies = []

    def block(src, lo, dst, col, n, row):
        copies.append(
            pltpu.make_async_copy(
                src.at[:, pl.ds(lo, n)],
                dst.at[pl.ds(row, 16), pl.ds(col, n)],
                sem.at[len(copies)],
            )
        )

    for k in range(4):
        for j in range(4):
            row = ((x - STEPS[j]) % 4 * 4 + (y - STEPS[k]) % 4) * 16
            block(first[k].at[j], 0, hidden.at[1], 0, WIDE, row)
            block(first[k].at[j], WIDE, hidden.at[2], 0, half, row)
            row = ((x - STEPS[k]) % 4 * 4 + (y - STEPS[j]) % 4) * 16
            block(second[k].at[j], 0, hidden.at[2], half, half, row)
            block(second[k].at[j], half, hidden.at[0], 0, WIDE, row)
    loads = []
    for h in range(2):
        for head, lo in ((heads[2 + h], 0), (heads[h], 0), (heads[h], WIDE)):
            n = len(loads)
            loads.append(
                pltpu.make_async_copy(
                    head.at[:, pl.ds(lo, WIDE)], held.at[n], sem.at[64 + n]
                )
            )
    for copy in copies + loads[:2]:
        copy.start()
    terms[...] = jnp.zeros_like(terms)
    for copy in copies:
        copy.wait()
    rows = pltpu.make_async_copy(hidden.at[0], rows_out, out_sem.at[0])
    rows.start()

    nt = NP * 16

    def finish(i):
        mine = terms.at[2 * i : 2 * i + 2]
        peak = jnp.max(jnp.max(mine[...], 0), 0, keepdims=True)
        value = jnp.exp(mine[...] - peak)
        mine[...] = value
        outs[i].start()
        total = jnp.sum(jnp.sum(value, 0), 0, keepdims=True)
        logs_out[:, i * nt : (i + 1) * nt] = peak + jnp.log(total)
        base_out[i : i + 1] = peak

    outs = [
        pltpu.make_async_copy(terms.at[2 * i : 2 * i + 2], out, out_sem.at[1 + i])
        for i, out in enumerate((stud_out, teach_out))
    ]

    @pl.loop(0, 6)
    def _(n):
        for i in range(6):

            @pl.when(n == i)
            def _():
                loads[i].wait()
                if i + 2 < 6:
                    loads[i + 2].start()

        j = n % 3
        terms[n // 3 + jnp.where(j > 0, 2, 0)] += lax.dot_general(
            held[n], hidden[j], (((1,), (1,)), ((), ())), preferred_element_type=jnp.float32
        )

        @pl.when(n == 3)
        def _():
            finish(0)

    finish(1)
    logs_out[:, 2 * nt :] = weight[...]
    rows.wait()
    for copy in outs:
        copy.wait()


def logits(at, weight, first, second, heads):
    ve, nt = heads[0].shape[0], NP * 16
    shape = jax.ShapeDtypeStruct
    return pl.pallas_call(
        logits_kernel,
        out_shape=[
            shape((2, ve, nt), jnp.float32),
            shape((2, ve, nt), jnp.float32),
            shape((nt, WIDE), jnp.bfloat16),
            shape((1, 3 * nt), jnp.float32),
            shape((2, nt), jnp.float32),
        ],
        in_specs=[SMEM, VMEM] + [HBM] * 12,
        out_specs=[HBM] * 3 + [VMEM] * 2,
        scratch_shapes=[
            pltpu.VMEM((3, nt, WIDE), jnp.bfloat16),
            pltpu.VMEM((6, ve, WIDE), jnp.bfloat16),
            pltpu.VMEM((4, ve, nt), jnp.float32),
            pltpu.SemaphoreType.DMA((70,)),
            pltpu.SemaphoreType.DMA((3,)),
        ],
        compiler_params=pltpu.CompilerParams(vmem_limit_bytes=VMEM_LIMIT),
        cost_estimate=pl.CostEstimate(
            flops=2 * 2 * ve * nt * 3 * WIDE,
            bytes_accessed=2 * ve * 3 * WIDE * 2 + nt * 3 * WIDE * 2,
            transcendentals=4 * ve * nt,
        ),
    )(at, weight, *first, *second, *heads)


def grad_kernel(teach, stud, head0, head1, rows, logs, base, *refs):
    ours_out, theirs_out, part_out = refs[:3]
    terms_t, terms_s, held, row, grad, theirs, sem, out_sem = refs[3:]
    pairs = []
    for h in (1, 0):
        pairs += [(stud.at[h], terms_s.at[h]), (teach.at[h], terms_t.at[h])]
    pairs.insert(2, (rows, row))
    pairs += [(head1, held.at[1]), (head0, held.at[0])]
    loads = [
        pltpu.make_async_copy(src, dst, sem.at[i]) for i, (src, dst) in enumerate(pairs)
    ]
    for copy in loads:
        copy.start()
    nt = base.shape[1]
    weight = logs[:, 2 * nt :]
    scale = [
        weight * jnp.exp(base[i : i + 1] - logs[:, i * nt : (i + 1) * nt]) for i in range(2)
    ]

    def gradient(h):
        grad[h] = (terms_s[h] * scale[0] - terms_t[h] * scale[1]).astype(jnp.bfloat16)

    loads[0].wait()
    loads[1].wait()
    gradient(1)
    loads[2].wait()

    @pl.loop(0, 4)
    def _(n):
        cols = pl.ds(pl.multiple_of(n * 512, 512), 512)
        theirs[:, cols] = jnp.dot(
            grad[1], row[:, cols], preferred_element_type=jnp.float32
        ).astype(theirs.dtype)

    outs = [pltpu.make_async_copy(theirs, theirs_out, out_sem.at[0])]
    outs[0].start()
    loads[3].wait()
    loads[4].wait()
    gradient(0)
    outs.append(pltpu.make_async_copy(grad.at[0], ours_out, out_sem.at[1]))
    outs[1].start()
    loads[5].wait()
    loads[6].wait()

    @pl.loop(0, 4)
    def _(n):
        cols = pl.ds(pl.multiple_of(n * 512, 512), 512)
        total = sum(
            lax.dot_general(
                grad[h],
                held[h, :, cols],
                (((0,), (0,)), ((), ())),
                preferred_element_type=jnp.float32,
            )
            for h in range(2)
        )
        part_out[:, cols] = total.astype(part_out.dtype)

    for copy in outs:
        copy.wait()


def grads(teach, stud, head0, head1, rows, logs, base):
    ve, nt = teach.shape[1:]
    shape = jax.ShapeDtypeStruct
    return pl.pallas_call(
        grad_kernel,
        out_shape=[
            shape((ve, nt), jnp.bfloat16),
            shape((ve, WIDE), jnp.bfloat16),
            shape((nt, WIDE), jnp.bfloat16),
        ],
        in_specs=[HBM] * 5 + [VMEM] * 2,
        out_specs=[HBM] * 2 + [VMEM],
        scratch_shapes=[
            pltpu.VMEM((2, ve, nt), jnp.float32),
            pltpu.VMEM((2, ve, nt), jnp.float32),
            pltpu.VMEM((2, ve, WIDE), jnp.bfloat16),
            pltpu.VMEM((nt, WIDE), jnp.bfloat16),
            pltpu.VMEM((2, ve, nt), jnp.bfloat16),
            pltpu.VMEM((ve, WIDE), jnp.bfloat16),
            pltpu.SemaphoreType.DMA((7,)),
            pltpu.SemaphoreType.DMA((2,)),
        ],
        compiler_params=pltpu.CompilerParams(vmem_limit_bytes=VMEM_LIMIT),
        cost_estimate=pl.CostEstimate(
            flops=3 * 2 * ve * nt * WIDE,
            bytes_accessed=2 * ve * WIDE * 2 + 2 * 2 * ve * nt * 4 + ve * WIDE * 2,
            transcendentals=0,
        ),
    )(teach, stud, head0, head1, rows, logs, base)


def on_device(teacher_hidden, student_hidden, teacher_head, student_head, loss_weight):
    tok, dt = teacher_hidden.shape
    ds = student_hidden.shape[1]
    nt = tok * NP * NL
    heads = (teacher_head, swap(teacher_head), student_head, swap(student_head))

    x, y = lax.axis_index("x"), lax.axis_index("y")
    mine = jnp.concatenate([teacher_hidden, student_hidden], 1)
    line = share(mine, LINE, NL).reshape(NL * tok, -1)
    line, heads = lax.optimization_barrier((line, heads))
    half = (dt + ds) // 2
    z = lax.axis_index("zl") * 4 + lax.axis_index("zh")
    weight = lax.dynamic_update_slice(
        jnp.zeros((1, nt), jnp.float32), loss_weight[None], (0, ((x * 4 + y) * NL + z) * tok)
    )
    second = ring(jnp.stack(ring(line[:, half:], "y")), "x")
    first = ring(jnp.stack(ring(line[:, :half], "x")), "y")
    teach, stud, rows, logs, base = logits(jnp.stack([x, y]), weight, first, second, heads)
    logs = join(share(join(share(logs, PLANE, NP), nt), LINE, NL), nt)
    grad, theirs, part = grads(teach, stud, heads[2], heads[3], rows, logs, base)

    theirs = swap(theirs)
    part = plane_sum(part.reshape(NP, NL * tok, ds), PLANE).reshape(NL, tok, ds)
    ours = jnp.dot(grad, rows, preferred_element_type=jnp.float32)
    part, ours, theirs = lax.optimization_barrier((part, ours, theirs))
    hidden_grad = plane_sum(part, LINE)
    return hidden_grad, (ours + theirs).astype(jnp.bfloat16)


def solution(mesh):
    fine = Mesh(mesh.devices.reshape(SIZES), AXES)
    split = P(AXES, None)
    return jax.shard_map(
        on_device,
        mesh=fine,
        in_specs=(split, split, split, split, P(AXES)),
        out_specs=(split, split),
        check_vma=False,
    )
```

```python
import jax
import jax.numpy as jnp
from jax import lax
from jax.experimental import pallas as pl
from jax.experimental.pallas import tpu as pltpu
from jax.sharding import Mesh, PartitionSpec as P

AXES = ("x", "zl", "y", "zh", "c")
SIZES = (4, 2, 4, 4, 2)
PLANE, LINE, PAIR = ("x", "y"), ("zl", "zh"), ("c",)
NP, NL = 16, 8
STEPS = (0, 1, 3, 2)
VMEM_LIMIT = 62 * 2**20
HBM, SMEM = pl.BlockSpec(memory_space=pltpu.HBM), pl.BlockSpec(memory_space=pltpu.SMEM)
VMEM = pl.BlockSpec(memory_space=pltpu.VMEM)
WIDE = 2048
FLIGHT = 4


def share(block, axes, n):
    return lax.all_to_all(
        jnp.broadcast_to(block[None], (n,) + block.shape), axes, 0, 0, tiled=True
    )


def ring(block, axis):
    return [block] + [
        lax.ppermute(block, axis, [(i, (i + step) % 4) for i in range(4)])
        for step in STEPS[1:]
    ]


def join(rows, nt):
    logs = rows[:, :, : 2 * nt]
    top = jnp.max(logs, 0)
    logs = top + jnp.log(jnp.sum(jnp.exp(logs - top), 0))
    return jnp.concatenate([logs, jnp.sum(rows[:, :, 2 * nt :], 0)], 1)


def plane_sum(blocks, axes):
    got = lax.all_to_all(blocks, axes, 0, 0, tiled=True)
    return jnp.sum(got.astype(jnp.float32), 0)


def swap(block):
    return lax.ppermute(block, PAIR, [(0, 1), (1, 0)])


def logits_kernel(at, weight, *refs):
    first, second = refs[:4], refs[4:8]
    heads = refs[8:12]
    teach_out, stud_out, rows_out, logs_out, base_out = refs[12:17]
    hidden, held, terms, sem, out_sem = refs[17:]
    x, y = at[0], at[1]
    half = WIDE // 2
    copies = []

    def block(src, lo, dst, col, n, row):
        copies.append(
            pltpu.make_async_copy(
                src.at[:, pl.ds(lo, n)],
                dst.at[pl.ds(row, 16), pl.ds(col, n)],
                sem.at[len(copies)],
            )
        )

    for k in range(4):
        for j in range(4):
            row = ((x - STEPS[j]) % 4 * 4 + (y - STEPS[k]) % 4) * 16
            block(first[k].at[j], 0, hidden.at[1], 0, WIDE, row)
            block(first[k].at[j], WIDE, hidden.at[2], 0, half, row)
            row = ((x - STEPS[k]) % 4 * 4 + (y - STEPS[j]) % 4) * 16
            block(second[k].at[j], 0, hidden.at[2], half, half, row)
            block(second[k].at[j], half, hidden.at[0], 0, WIDE, row)
    loads = []
    for h in range(2):
        for head, lo in ((heads[2 + h], 0), (heads[h], 0), (heads[h], WIDE)):
            n = len(loads)
            loads.append(
                pltpu.make_async_copy(
                    head.at[:, pl.ds(lo, WIDE)], held.at[n], sem.at[64 + n]
                )
            )
    for copy in copies + loads[:FLIGHT]:
        copy.start()
    terms[...] = jnp.zeros_like(terms)
    for copy in copies:
        copy.wait()
    rows = pltpu.make_async_copy(hidden.at[0], rows_out, out_sem.at[0])
    rows.start()

    nt = NP * 16

    def finish(i):
        mine = terms.at[2 * i : 2 * i + 2]
        peak = jnp.max(jnp.max(mine[...], 0), 0, keepdims=True)
        value = jnp.exp(mine[...] - peak)
        mine[...] = value
        outs[i].start()
        total = jnp.sum(jnp.sum(value, 0), 0, keepdims=True)
        logs_out[:, :, i * nt : (i + 1) * nt] = jnp.broadcast_to(
            peak + jnp.log(total), (NP, 1, nt)
        )
        base_out[i : i + 1] = peak

    outs = [
        pltpu.make_async_copy(terms.at[2 * i : 2 * i + 2], out, out_sem.at[1 + i])
        for i, out in enumerate((stud_out, teach_out))
    ]

    @pl.loop(0, 6)
    def _(n):
        for i in range(6):

            @pl.when(n == i)
            def _():
                loads[i].wait()
                if i + FLIGHT < 6:
                    loads[i + FLIGHT].start()

        j = n % 3
        terms[n // 3 + jnp.where(j > 0, 2, 0)] += lax.dot_general(
            held[n], hidden[j], (((1,), (1,)), ((), ())), preferred_element_type=jnp.float32
        )

        @pl.when(n == 3)
        def _():
            finish(0)

    finish(1)
    logs_out[:, :, 2 * nt :] = jnp.broadcast_to(weight[...], (NP, 1, nt))
    rows.wait()
    for copy in outs:
        copy.wait()


def logits(at, weight, first, second, heads):
    ve, nt = heads[0].shape[0], NP * 16
    shape = jax.ShapeDtypeStruct
    return pl.pallas_call(
        logits_kernel,
        out_shape=[
            shape((2, ve, nt), jnp.float32),
            shape((2, ve, nt), jnp.float32),
            shape((nt, WIDE), jnp.bfloat16),
            shape((NP, 1, 3 * nt), jnp.float32),
            shape((2, nt), jnp.float32),
        ],
        in_specs=[SMEM, VMEM] + [HBM] * 12,
        out_specs=[HBM] * 3 + [VMEM] * 2,
        scratch_shapes=[
            pltpu.VMEM((3, nt, WIDE), jnp.bfloat16),
            pltpu.VMEM((6, ve, WIDE), jnp.bfloat16),
            pltpu.VMEM((4, ve, nt), jnp.float32),
            pltpu.SemaphoreType.DMA((70,)),
            pltpu.SemaphoreType.DMA((3,)),
        ],
        compiler_params=pltpu.CompilerParams(vmem_limit_bytes=VMEM_LIMIT),
        cost_estimate=pl.CostEstimate(
            flops=2 * 2 * ve * nt * 3 * WIDE,
            bytes_accessed=2 * ve * 3 * WIDE * 2 + nt * 3 * WIDE * 2,
            transcendentals=4 * ve * nt,
        ),
    )(at, weight, *first, *second, *heads)


def grad_kernel(teach, stud, head0, head1, rows, logs, base, *refs):
    ours_out, theirs_out, part_out = refs[:3]
    terms_t, terms_s, held, row, grad, theirs, sem, out_sem = refs[3:]
    pairs = []
    for h in (1, 0):
        pairs += [(stud.at[h], terms_s.at[h]), (teach.at[h], terms_t.at[h])]
    pairs.insert(2, (rows, row))
    pairs += [(head1, held.at[1]), (head0, held.at[0])]
    loads = [
        pltpu.make_async_copy(src, dst, sem.at[i]) for i, (src, dst) in enumerate(pairs)
    ]
    for copy in loads:
        copy.start()
    nt = base.shape[1]
    every = join(logs[...], nt)
    weight = every[:, 2 * nt :]
    scale = [
        weight * jnp.exp(base[i : i + 1] - every[:, i * nt : (i + 1) * nt]) for i in range(2)
    ]

    def gradient(h):
        grad[h] = (terms_s[h] * scale[0] - terms_t[h] * scale[1]).astype(jnp.bfloat16)

    loads[0].wait()
    loads[1].wait()
    gradient(1)
    loads[2].wait()

    @pl.loop(0, 4)
    def _(n):
        cols = pl.ds(pl.multiple_of(n * 512, 512), 512)
        theirs[:, cols] = jnp.dot(
            grad[1], row[:, cols], preferred_element_type=jnp.float32
        ).astype(theirs.dtype)

    outs = [pltpu.make_async_copy(theirs, theirs_out, out_sem.at[0])]
    outs[0].start()
    loads[3].wait()
    loads[4].wait()
    gradient(0)
    outs.append(pltpu.make_async_copy(grad.at[0], ours_out, out_sem.at[1]))
    outs[1].start()
    loads[5].wait()
    loads[6].wait()

    @pl.loop(0, 4)
    def _(n):
        cols = pl.ds(pl.multiple_of(n * 512, 512), 512)
        total = sum(
            lax.dot_general(
                grad[h],
                held[h, :, cols],
                (((0,), (0,)), ((), ())),
                preferred_element_type=jnp.float32,
            )
            for h in range(2)
        )
        part_out[:, cols] = total.astype(part_out.dtype)

    for copy in outs:
        copy.wait()


def grads(teach, stud, head0, head1, rows, logs, base):
    ve, nt = teach.shape[1:]
    shape = jax.ShapeDtypeStruct
    return pl.pallas_call(
        grad_kernel,
        out_shape=[
            shape((ve, nt), jnp.bfloat16),
            shape((ve, WIDE), jnp.bfloat16),
            shape((nt, WIDE), jnp.bfloat16),
        ],
        in_specs=[HBM] * 5 + [VMEM] * 2,
        out_specs=[HBM] * 2 + [VMEM],
        scratch_shapes=[
            pltpu.VMEM((2, ve, nt), jnp.float32),
            pltpu.VMEM((2, ve, nt), jnp.float32),
            pltpu.VMEM((2, ve, WIDE), jnp.bfloat16),
            pltpu.VMEM((nt, WIDE), jnp.bfloat16),
            pltpu.VMEM((2, ve, nt), jnp.bfloat16),
            pltpu.VMEM((ve, WIDE), jnp.bfloat16),
            pltpu.SemaphoreType.DMA((7,)),
            pltpu.SemaphoreType.DMA((2,)),
        ],
        compiler_params=pltpu.CompilerParams(vmem_limit_bytes=VMEM_LIMIT),
        cost_estimate=pl.CostEstimate(
            flops=3 * 2 * ve * nt * WIDE,
            bytes_accessed=2 * ve * WIDE * 2 + 2 * 2 * ve * nt * 4 + ve * WIDE * 2,
            transcendentals=0,
        ),
    )(teach, stud, head0, head1, rows, logs, base)


def on_device(teacher_hidden, student_hidden, teacher_head, student_head, loss_weight):
    tok, dt = teacher_hidden.shape
    ds = student_hidden.shape[1]
    nt = tok * NP * NL
    heads = (teacher_head, swap(teacher_head), student_head, swap(student_head))

    x, y = lax.axis_index("x"), lax.axis_index("y")
    mine = jnp.concatenate([teacher_hidden, student_hidden], 1)
    line = share(mine, LINE, NL).reshape(NL * tok, -1)
    line, heads = lax.optimization_barrier((line, heads))
    half = (dt + ds) // 2
    z = lax.axis_index("zl") * 4 + lax.axis_index("zh")
    weight = lax.dynamic_update_slice(
        jnp.zeros((1, nt), jnp.float32), loss_weight[None], (0, ((x * 4 + y) * NL + z) * tok)
    )
    second = ring(jnp.stack(ring(line[:, half:], "y")), "x")
    first = ring(jnp.stack(ring(line[:, :half], "x")), "y")
    teach, stud, rows, logs, base = logits(jnp.stack([x, y]), weight, first, second, heads)
    logs = join(lax.all_to_all(logs, PLANE, 0, 0, tiled=True), nt)
    logs = share(logs, LINE, NL)
    grad, theirs, part = grads(teach, stud, heads[2], heads[3], rows, logs, base)

    theirs = swap(theirs)
    part = plane_sum(part.reshape(NP, NL * tok, ds), PLANE).reshape(NL, tok, ds)
    ours = jnp.dot(grad, rows, preferred_element_type=jnp.float32)
    part, ours, theirs = lax.optimization_barrier((part, ours, theirs))
    hidden_grad = plane_sum(part, LINE)
    return hidden_grad, (ours + theirs).astype(jnp.bfloat16)


def solution(mesh):
    fine = Mesh(mesh.devices.reshape(SIZES), AXES)
    split = P(AXES, None)
    return jax.shard_map(
        on_device,
        mesh=fine,
        in_specs=(split, split, split, split, P(AXES)),
        out_specs=(split, split),
        check_vma=False,
    )
```

```python
import jax
import jax.numpy as jnp
from jax import lax
from jax.experimental import pallas as pl
from jax.experimental.pallas import tpu as pltpu
from jax.sharding import Mesh, PartitionSpec as P

AXES = ("x", "zl", "y", "zh", "c")
SIZES = (4, 2, 4, 4, 2)
PLANE, LINE, PAIR = ("x", "y"), ("zl", "zh"), ("c",)
NP, NL = 16, 8
STEPS = (0, 1, 3, 2)
VMEM_LIMIT = 62 * 2**20
HBM, SMEM = pl.BlockSpec(memory_space=pltpu.HBM), pl.BlockSpec(memory_space=pltpu.SMEM)
VMEM = pl.BlockSpec(memory_space=pltpu.VMEM)
WIDE = 2048
FLIGHT = 4


def share(block, axes, n):
    return lax.all_to_all(
        jnp.broadcast_to(block[None], (n,) + block.shape), axes, 0, 0, tiled=True
    )


def ring(block, axis):
    return [block] + [
        lax.ppermute(block, axis, [(i, (i + step) % 4) for i in range(4)])
        for step in STEPS[1:]
    ]


def join(rows, nt):
    logs = rows[:, :, : 2 * nt]
    top = jnp.max(logs, 0)
    logs = top + jnp.log(jnp.sum(jnp.exp(logs - top), 0))
    return jnp.concatenate([logs, jnp.sum(rows[:, :, 2 * nt :], 0)], 1)


def plane_sum(blocks, axes):
    got = lax.all_to_all(blocks, axes, 0, 0, tiled=True)
    return jnp.sum(got.astype(jnp.float32), 0)


def swap(block):
    return lax.ppermute(block, PAIR, [(0, 1), (1, 0)])


def logits_kernel(at, weight, *refs):
    first, second = refs[:4], refs[4:8]
    heads = refs[8:12]
    teach_out, stud_out, rows_out, logs_out, base_out = refs[12:17]
    hidden, held, terms, sem, out_sem = refs[17:]
    x, y = at[0], at[1]
    half = WIDE // 2
    copies = []

    def block(src, lo, dst, col, n, row):
        copies.append(
            pltpu.make_async_copy(
                src.at[:, pl.ds(lo, n)],
                dst.at[pl.ds(row, 16), pl.ds(col, n)],
                sem.at[len(copies)],
            )
        )

    for k in range(4):
        for j in range(4):
            row = ((x - STEPS[j]) % 4 * 4 + (y - STEPS[k]) % 4) * 16
            block(first[k].at[j], 0, hidden.at[1], 0, WIDE, row)
            block(first[k].at[j], WIDE, hidden.at[2], 0, half, row)
            row = ((x - STEPS[k]) % 4 * 4 + (y - STEPS[j]) % 4) * 16
            block(second[k].at[j], 0, hidden.at[2], half, half, row)
            block(second[k].at[j], half, hidden.at[0], 0, WIDE, row)
    loads = []
    for h in range(2):
        for head, lo in ((heads[2 + h], 0), (heads[h], 0), (heads[h], WIDE)):
            n = len(loads)
            loads.append(
                pltpu.make_async_copy(
                    head.at[:, pl.ds(lo, WIDE)], held.at[n], sem.at[64 + n]
                )
            )
    for copy in copies + loads[:FLIGHT]:
        copy.start()
    terms[...] = jnp.zeros_like(terms)
    for copy in copies:
        copy.wait()
    rows = pltpu.make_async_copy(hidden.at[0], rows_out, out_sem.at[0])
    rows.start()

    nt = NP * 16

    def finish(i):
        mine = terms.at[2 * i : 2 * i + 2]
        peak = jnp.max(jnp.max(mine[...], 0), 0, keepdims=True)
        value = jnp.exp(mine[...] - peak)
        mine[...] = value
        outs[i].start()
        total = jnp.sum(jnp.sum(value, 0), 0, keepdims=True)
        logs_out[:, :, i * nt : (i + 1) * nt] = jnp.broadcast_to(
            peak + jnp.log(total), (NP, 1, nt)
        )
        base_out[i : i + 1] = peak

    outs = [
        pltpu.make_async_copy(terms.at[2 * i : 2 * i + 2], out, out_sem.at[1 + i])
        for i, out in enumerate((stud_out, teach_out))
    ]

    @pl.loop(0, 6)
    def _(n):
        for i in range(6):

            @pl.when(n == i)
            def _():
                loads[i].wait()
                if i + FLIGHT < 6:
                    loads[i + FLIGHT].start()

        j = n % 3
        terms[n // 3 + jnp.where(j > 0, 2, 0)] += lax.dot_general(
            held[n], hidden[j], (((1,), (1,)), ((), ())), preferred_element_type=jnp.float32
        )

        @pl.when(n == 3)
        def _():
            finish(0)

    finish(1)
    logs_out[:, :, 2 * nt :] = jnp.broadcast_to(weight[...], (NP, 1, nt))
    rows.wait()
    for copy in outs:
        copy.wait()


def logits(at, weight, first, second, heads):
    ve, nt = heads[0].shape[0], NP * 16
    shape = jax.ShapeDtypeStruct
    return pl.pallas_call(
        logits_kernel,
        out_shape=[
            shape((2, ve, nt), jnp.float32),
            shape((2, ve, nt), jnp.float32),
            shape((nt, WIDE), jnp.bfloat16),
            shape((NP, 1, 3 * nt), jnp.float32),
            shape((2, nt), jnp.float32),
        ],
        in_specs=[SMEM, VMEM] + [HBM] * 12,
        out_specs=[HBM] * 3 + [VMEM] * 2,
        scratch_shapes=[
            pltpu.VMEM((3, nt, WIDE), jnp.bfloat16),
            pltpu.VMEM((6, ve, WIDE), jnp.bfloat16),
            pltpu.VMEM((4, ve, nt), jnp.float32),
            pltpu.SemaphoreType.DMA((70,)),
            pltpu.SemaphoreType.DMA((3,)),
        ],
        compiler_params=pltpu.CompilerParams(vmem_limit_bytes=VMEM_LIMIT),
        cost_estimate=pl.CostEstimate(
            flops=2 * 2 * ve * nt * 3 * WIDE,
            bytes_accessed=2 * ve * 3 * WIDE * 2 + nt * 3 * WIDE * 2,
            transcendentals=4 * ve * nt,
        ),
    )(at, weight, *first, *second, *heads)


def grad_kernel(teach, stud, head0, head1, rows, logs, base, *refs):
    ours_out, part_out, *theirs_out = refs[:6]
    terms_t, terms_s, held, row, grad, theirs, sem, out_sem = refs[6:]
    pairs = []
    for h in (1, 0):
        pairs += [(stud.at[h], terms_s.at[h]), (teach.at[h], terms_t.at[h])]
    pairs.insert(2, (rows, row))
    pairs += [(head1, held.at[1]), (head0, held.at[0])]
    loads = [
        pltpu.make_async_copy(src, dst, sem.at[i]) for i, (src, dst) in enumerate(pairs)
    ]
    for copy in loads:
        copy.start()
    nt = base.shape[1]
    every = join(logs[...], nt)
    weight = every[:, 2 * nt :]
    scale = [
        weight * jnp.exp(base[i : i + 1] - every[:, i * nt : (i + 1) * nt]) for i in range(2)
    ]

    def gradient(h):
        grad[h] = (terms_s[h] * scale[0] - terms_t[h] * scale[1]).astype(jnp.bfloat16)

    loads[0].wait()
    loads[1].wait()
    gradient(1)
    loads[2].wait()

    @pl.loop(0, 4)
    def _(n):
        cols = pl.ds(pl.multiple_of(n * 512, 512), 512)
        theirs[n] = jnp.dot(
            grad[1], row[:, cols], preferred_element_type=jnp.float32
        ).astype(theirs.dtype)

    outs = [
        pltpu.make_async_copy(theirs.at[i], out, out_sem.at[1 + i])
        for i, out in enumerate(theirs_out)
    ]
    for copy in outs:
        copy.start()
    loads[3].wait()
    loads[4].wait()
    gradient(0)
    outs.append(pltpu.make_async_copy(grad.at[0], ours_out, out_sem.at[0]))
    outs[-1].start()
    loads[5].wait()
    loads[6].wait()

    @pl.loop(0, 4)
    def _(n):
        cols = pl.ds(pl.multiple_of(n * 512, 512), 512)
        total = sum(
            lax.dot_general(
                grad[h],
                held[h, :, cols],
                (((0,), (0,)), ((), ())),
                preferred_element_type=jnp.float32,
            )
            for h in range(2)
        )
        part_out[:, cols] = total.astype(part_out.dtype)

    for copy in outs:
        copy.wait()


def grads(teach, stud, head0, head1, rows, logs, base):
    ve, nt = teach.shape[1:]
    shape = jax.ShapeDtypeStruct
    return pl.pallas_call(
        grad_kernel,
        out_shape=[
            shape((ve, nt), jnp.bfloat16),
            shape((nt, WIDE), jnp.bfloat16),
        ]
        + [shape((ve, WIDE // 4), jnp.bfloat16)] * 4,
        in_specs=[HBM] * 5 + [VMEM] * 2,
        out_specs=[HBM, VMEM] + [HBM] * 4,
        scratch_shapes=[
            pltpu.VMEM((2, ve, nt), jnp.float32),
            pltpu.VMEM((2, ve, nt), jnp.float32),
            pltpu.VMEM((2, ve, WIDE), jnp.bfloat16),
            pltpu.VMEM((nt, WIDE), jnp.bfloat16),
            pltpu.VMEM((2, ve, nt), jnp.bfloat16),
            pltpu.VMEM((4, ve, WIDE // 4), jnp.bfloat16),
            pltpu.SemaphoreType.DMA((7,)),
            pltpu.SemaphoreType.DMA((5,)),
        ],
        compiler_params=pltpu.CompilerParams(vmem_limit_bytes=VMEM_LIMIT),
        cost_estimate=pl.CostEstimate(
            flops=3 * 2 * ve * nt * WIDE,
            bytes_accessed=2 * ve * WIDE * 2 + 2 * 2 * ve * nt * 4 + ve * WIDE * 2,
            transcendentals=0,
        ),
    )(teach, stud, head0, head1, rows, logs, base)


def on_device(teacher_hidden, student_hidden, teacher_head, student_head, loss_weight):
    tok, dt = teacher_hidden.shape
    ds = student_hidden.shape[1]
    nt = tok * NP * NL
    heads = (teacher_head, swap(teacher_head), student_head, swap(student_head))

    x, y = lax.axis_index("x"), lax.axis_index("y")
    mine = jnp.concatenate([teacher_hidden, student_hidden], 1)
    line = share(mine, LINE, NL).reshape(NL * tok, -1)
    line, heads = lax.optimization_barrier((line, heads))
    half = (dt + ds) // 2
    z = lax.axis_index("zl") * 4 + lax.axis_index("zh")
    weight = lax.dynamic_update_slice(
        jnp.zeros((1, nt), jnp.float32), loss_weight[None], (0, ((x * 4 + y) * NL + z) * tok)
    )
    second = ring(jnp.stack(ring(line[:, half:], "y")), "x")
    first = ring(jnp.stack(ring(line[:, :half], "x")), "y")
    teach, stud, rows, logs, base = logits(jnp.stack([x, y]), weight, first, second, heads)
    logs = join(lax.all_to_all(logs, PLANE, 0, 0, tiled=True), nt)
    logs = share(logs, LINE, NL)
    grad, part, *theirs = grads(teach, stud, heads[2], heads[3], rows, logs, base)

    theirs = jnp.concatenate([swap(block) for block in theirs], 1)
    part = plane_sum(part.reshape(NP, NL * tok, ds), PLANE).reshape(NL, tok, ds)
    ours = jnp.dot(grad, rows, preferred_element_type=jnp.float32)
    part, ours, theirs = lax.optimization_barrier((part, ours, theirs))
    hidden_grad = plane_sum(part, LINE)
    return hidden_grad, (ours + theirs).astype(jnp.bfloat16)


def solution(mesh):
    fine = Mesh(mesh.devices.reshape(SIZES), AXES)
    split = P(AXES, None)
    return jax.shard_map(
        on_device,
        mesh=fine,
        in_specs=(split, split, split, split, P(AXES)),
        out_specs=(split, split),
        check_vma=False,
    )
```

```python
import jax
import jax.numpy as jnp
from jax import lax
from jax.experimental import pallas as pl
from jax.experimental.pallas import tpu as pltpu
from jax.sharding import Mesh, PartitionSpec as P

AXES = ("x", "zl", "y", "zh", "c")
SIZES = (4, 2, 4, 4, 2)
PLANE, LINE, PAIR = ("x", "y"), ("zl", "zh"), ("c",)
NP, NL = 16, 8
STEPS = (0, 3, 1, 2)
VMEM_LIMIT = 62 * 2**20
HBM, SMEM = pl.BlockSpec(memory_space=pltpu.HBM), pl.BlockSpec(memory_space=pltpu.SMEM)
VMEM = pl.BlockSpec(memory_space=pltpu.VMEM)
WIDE = 2048
FLIGHT = 4


def share(block, axes, n):
    return lax.all_to_all(
        jnp.broadcast_to(block[None], (n,) + block.shape), axes, 0, 0, tiled=True
    )


def ring(block, axis):
    return [block] + [
        lax.ppermute(block, axis, [(i, (i + step) % 4) for i in range(4)])
        for step in STEPS[1:]
    ]


def join(rows, nt):
    logs = rows[:, :, : 2 * nt]
    top = jnp.max(logs, 0)
    logs = top + jnp.log(jnp.sum(jnp.exp(logs - top), 0))
    return jnp.concatenate([logs, jnp.sum(rows[:, :, 2 * nt :], 0)], 1)


def plane_sum(blocks, axes):
    got = lax.all_to_all(blocks, axes, 0, 0, tiled=True)
    return jnp.sum(got.astype(jnp.float32), 0)


def swap(block):
    return lax.ppermute(block, PAIR, [(0, 1), (1, 0)])


def logits_kernel(at, weight, *refs):
    first, second = refs[:4], refs[4:8]
    heads = refs[8:12]
    teach_out, stud_out, rows_out, logs_out, base_out = refs[12:17]
    hidden, held, terms, sem, out_sem = refs[17:]
    x, y = at[0], at[1]
    half = WIDE // 2
    copies = []

    def block(src, lo, dst, col, n, row):
        copies.append(
            pltpu.make_async_copy(
                src.at[:, pl.ds(lo, n)],
                dst.at[pl.ds(row, 16), pl.ds(col, n)],
                sem.at[len(copies)],
            )
        )

    for k in range(4):
        for j in range(4):
            row = ((x - STEPS[j]) % 4 * 4 + (y - STEPS[k]) % 4) * 16
            block(first[k].at[j], 0, hidden.at[1], 0, WIDE, row)
            block(first[k].at[j], WIDE, hidden.at[2], 0, half, row)
            row = ((x - STEPS[k]) % 4 * 4 + (y - STEPS[j]) % 4) * 16
            block(second[k].at[j], 0, hidden.at[2], half, half, row)
            block(second[k].at[j], half, hidden.at[0], 0, WIDE, row)
    loads = []
    for h in range(2):
        for head, lo in ((heads[2 + h], 0), (heads[h], 0), (heads[h], WIDE)):
            n = len(loads)
            loads.append(
                pltpu.make_async_copy(
                    head.at[:, pl.ds(lo, WIDE)], held.at[n], sem.at[64 + n]
                )
            )
    for copy in copies + loads[:FLIGHT]:
        copy.start()
    terms[...] = jnp.zeros_like(terms)
    for copy in copies:
        copy.wait()
    rows = pltpu.make_async_copy(hidden.at[0], rows_out, out_sem.at[0])
    rows.start()

    nt = NP * 16

    def finish(i):
        mine = terms.at[2 * i : 2 * i + 2]
        peak = jnp.max(jnp.max(mine[...], 0), 0, keepdims=True)
        value = jnp.exp(mine[...] - peak)
        mine[...] = value
        outs[i].start()
        total = jnp.sum(jnp.sum(value, 0), 0, keepdims=True)
        logs_out[:, :, i * nt : (i + 1) * nt] = jnp.broadcast_to(
            peak + jnp.log(total), (NP, 1, nt)
        )
        base_out[i : i + 1] = peak

    outs = [
        pltpu.make_async_copy(terms.at[2 * i : 2 * i + 2], out, out_sem.at[1 + i])
        for i, out in enumerate((stud_out, teach_out))
    ]

    @pl.loop(0, 6)
    def _(n):
        for i in range(6):

            @pl.when(n == i)
            def _():
                loads[i].wait()
                if i + FLIGHT < 6:
                    loads[i + FLIGHT].start()

        j = n % 3
        terms[n // 3 + jnp.where(j > 0, 2, 0)] += lax.dot_general(
            held[n], hidden[j], (((1,), (1,)), ((), ())), preferred_element_type=jnp.float32
        )

        @pl.when(n == 3)
        def _():
            finish(0)

    finish(1)
    logs_out[:, :, 2 * nt :] = jnp.broadcast_to(weight[...], (NP, 1, nt))
    rows.wait()
    for copy in outs:
        copy.wait()


def logits(at, weight, first, second, heads):
    ve, nt = heads[0].shape[0], NP * 16
    shape = jax.ShapeDtypeStruct
    return pl.pallas_call(
        logits_kernel,
        out_shape=[
            shape((2, ve, nt), jnp.float32),
            shape((2, ve, nt), jnp.float32),
            shape((nt, WIDE), jnp.bfloat16),
            shape((NP, 1, 3 * nt), jnp.float32),
            shape((2, nt), jnp.float32),
        ],
        in_specs=[SMEM, VMEM] + [HBM] * 12,
        out_specs=[HBM] * 3 + [VMEM] * 2,
        scratch_shapes=[
            pltpu.VMEM((3, nt, WIDE), jnp.bfloat16),
            pltpu.VMEM((6, ve, WIDE), jnp.bfloat16),
            pltpu.VMEM((4, ve, nt), jnp.float32),
            pltpu.SemaphoreType.DMA((70,)),
            pltpu.SemaphoreType.DMA((3,)),
        ],
        compiler_params=pltpu.CompilerParams(vmem_limit_bytes=VMEM_LIMIT),
        cost_estimate=pl.CostEstimate(
            flops=2 * 2 * ve * nt * 3 * WIDE,
            bytes_accessed=2 * ve * 3 * WIDE * 2 + nt * 3 * WIDE * 2,
            transcendentals=4 * ve * nt,
        ),
    )(at, weight, *first, *second, *heads)


def grad_kernel(teach, stud, head0, head1, rows, logs, base, *refs):
    ours_out, part_out, *theirs_out = refs[:6]
    terms_t, terms_s, held, row, grad, theirs, sem, out_sem = refs[6:]
    pairs = []
    for h in (1, 0):
        pairs += [(stud.at[h], terms_s.at[h]), (teach.at[h], terms_t.at[h])]
    pairs.insert(2, (rows, row))
    pairs += [(head1, held.at[1]), (head0, held.at[0])]
    loads = [
        pltpu.make_async_copy(src, dst, sem.at[i]) for i, (src, dst) in enumerate(pairs)
    ]
    for copy in loads:
        copy.start()
    nt = base.shape[1]
    every = join(logs[...], nt)
    weight = every[:, 2 * nt :]
    scale = [
        weight * jnp.exp(base[i : i + 1] - every[:, i * nt : (i + 1) * nt]) for i in range(2)
    ]

    def gradient(h):
        grad[h] = (terms_s[h] * scale[0] - terms_t[h] * scale[1]).astype(jnp.bfloat16)

    loads[0].wait()
    loads[1].wait()
    gradient(1)
    loads[2].wait()

    @pl.loop(0, 4)
    def _(n):
        cols = pl.ds(pl.multiple_of(n * 512, 512), 512)
        theirs[n] = jnp.dot(
            grad[1], row[:, cols], preferred_element_type=jnp.float32
        ).astype(theirs.dtype)

    outs = [
        pltpu.make_async_copy(theirs.at[i], out, out_sem.at[1 + i])
        for i, out in enumerate(theirs_out)
    ]
    for copy in outs:
        copy.start()
    loads[3].wait()
    loads[4].wait()
    gradient(0)
    outs.append(pltpu.make_async_copy(grad.at[0], ours_out, out_sem.at[0]))
    outs[-1].start()
    loads[5].wait()
    loads[6].wait()

    @pl.loop(0, 4)
    def _(n):
        cols = pl.ds(pl.multiple_of(n * 512, 512), 512)
        total = sum(
            lax.dot_general(
                grad[h],
                held[h, :, cols],
                (((0,), (0,)), ((), ())),
                preferred_element_type=jnp.float32,
            )
            for h in range(2)
        )
        part_out[:, cols] = total.astype(part_out.dtype)

    for copy in outs:
        copy.wait()


def grads(teach, stud, head0, head1, rows, logs, base):
    ve, nt = teach.shape[1:]
    shape = jax.ShapeDtypeStruct
    return pl.pallas_call(
        grad_kernel,
        out_shape=[
            shape((ve, nt), jnp.bfloat16),
            shape((nt, WIDE), jnp.bfloat16),
        ]
        + [shape((ve, WIDE // 4), jnp.bfloat16)] * 4,
        in_specs=[HBM] * 5 + [VMEM] * 2,
        out_specs=[HBM, VMEM] + [HBM] * 4,
        scratch_shapes=[
            pltpu.VMEM((2, ve, nt), jnp.float32),
            pltpu.VMEM((2, ve, nt), jnp.float32),
            pltpu.VMEM((2, ve, WIDE), jnp.bfloat16),
            pltpu.VMEM((nt, WIDE), jnp.bfloat16),
            pltpu.VMEM((2, ve, nt), jnp.bfloat16),
            pltpu.VMEM((4, ve, WIDE // 4), jnp.bfloat16),
            pltpu.SemaphoreType.DMA((7,)),
            pltpu.SemaphoreType.DMA((5,)),
        ],
        compiler_params=pltpu.CompilerParams(vmem_limit_bytes=VMEM_LIMIT),
        cost_estimate=pl.CostEstimate(
            flops=3 * 2 * ve * nt * WIDE,
            bytes_accessed=2 * ve * WIDE * 2 + 2 * 2 * ve * nt * 4 + ve * WIDE * 2,
            transcendentals=0,
        ),
    )(teach, stud, head0, head1, rows, logs, base)


def on_device(teacher_hidden, student_hidden, teacher_head, student_head, loss_weight):
    tok, dt = teacher_hidden.shape
    ds = student_hidden.shape[1]
    nt = tok * NP * NL
    heads = (teacher_head, swap(teacher_head), student_head, swap(student_head))

    x, y = lax.axis_index("x"), lax.axis_index("y")
    mine = jnp.concatenate([teacher_hidden, student_hidden], 1)
    line = share(mine, LINE, NL).reshape(NL * tok, -1)
    line, heads = lax.optimization_barrier((line, heads))
    half = (dt + ds) // 2
    z = lax.axis_index("zl") * 4 + lax.axis_index("zh")
    weight = lax.dynamic_update_slice(
        jnp.zeros((1, nt), jnp.float32), loss_weight[None], (0, ((x * 4 + y) * NL + z) * tok)
    )
    second = ring(jnp.stack(ring(line[:, half:], "y")), "x")
    first = ring(jnp.stack(ring(line[:, :half], "x")), "y")
    teach, stud, rows, logs, base = logits(jnp.stack([x, y]), weight, first, second, heads)
    logs = join(lax.all_to_all(logs, PLANE, 0, 0, tiled=True), nt)
    logs = share(logs, LINE, NL)
    grad, part, *theirs = grads(teach, stud, heads[2], heads[3], rows, logs, base)

    theirs = jnp.concatenate([swap(block) for block in theirs], 1)
    part = plane_sum(part.reshape(NP, NL * tok, ds), PLANE).reshape(NL, tok, ds)
    ours = jnp.dot(grad, rows, preferred_element_type=jnp.float32)
    part, ours, theirs = lax.optimization_barrier((part, ours, theirs))
    hidden_grad = plane_sum(part, LINE)
    return hidden_grad, (ours + theirs).astype(jnp.bfloat16)


def solution(mesh):
    fine = Mesh(mesh.devices.reshape(SIZES), AXES)
    split = P(AXES, None)
    return jax.shard_map(
        on_device,
        mesh=fine,
        in_specs=(split, split, split, split, P(AXES)),
        out_specs=(split, split),
        check_vma=False,
    )
```
